32 devices in a mesh: member: 2 (over y), gx: 16 (over z, x, core).
Axes of the slice: x: 2, y: 2, z: 4, core: 2. Of those that a mesh axis runs over, the one named last changes fastest.
Arguments:
- tracer: float32 [96, 96, 1536], P('member', 'gx'), parts along dimension 0, may hold values from -6 to 6
- frac_x: bfloat16 [96, 96, 1536], P('member', 'gx'), parts along dimension 0, may hold values from 0 to 1
- frac_y: bfloat16 [96, 96, 1536], P('member', 'gx'), parts along dimension 0, may hold values from 0 to 1
- vertical_modes: float32 [48, 48], replicated, may hold values from -0.875 to 0.875
- mode_projection: float32 [48, 48], replicated, may hold values from -0.875 to 0.875
- mode_rates: float32 [48], replicated, may hold values from 1 to 40
Outputs:
- updated: float32 [96, 96, 1536], P('member', 'gx'), parts along dimension 0
The draws below stay inside these ranges and needn't reach their ends.
There are 2 independent parts, one for each index of `member`. The reference program is written for one: setup_inputs(seed, part) draws one part's arguments, and reference() takes and returns one part's arrays. A program takes and returns all parts, laid end to end along the dimension named above; an argument that names none is the same for every part. Nothing has to cross between parts.
All inputs are finite; a program needn't handle non-finite values.
Results may differ from the reference program's by a relative error of at most 0.0003.
Values sent between devices are 32-bit elements; how exact they have to be, the bound alone decides.
A program may use at most 128 MiB of HBM per device.

```python
import math
import jax
import jax.numpy as jnp
from jax import lax

LEV = 48
NY = 1536
NX = 96
KY = 768
KX = 48


def steps_of(rng, shape, shards, least, top_value):
    gain, own = 1.0, jax.random.fold_in(rng, 6)
    for axis_at, shards_of in shards:
        draws = jnp.exp(jax.random.uniform(jax.random.fold_in(own, axis_at), (shards_of,), jnp.float32, least / len(shards), top_value / len(shards)))
        gain = gain * jnp.repeat(draws, shape[axis_at] // shards_of).reshape([-1 if axis == axis_at else 1 for axis in range(len(shape))])
    return gain


def bell_draw(own_key, shape, deviation, most, cuts=(), kind=jnp.bfloat16):
    values = deviation * jax.random.normal(own_key, shape, jnp.float32)
    if cuts:
        values = values * steps_of(own_key, shape, cuts, -0.22, 0.18)
    return jnp.clip(values, -most, most).astype(kind)


def setup_inputs(seed: int = 0, part: int = 0) -> dict:
    key_list = jax.random.split(jax.random.key(seed), 7)
    own_keys = jax.random.split(jax.random.fold_in(key_list[6], part), 7)
    tracer = bell_draw(own_keys[0], (LEV, NX, NY), 1.0, 6.0, ((1, 16),), jnp.float32)
    frac_x = jnp.clip(1.0 * jax.random.uniform(own_keys[1], (LEV, NX, NY), jnp.float32) ** steps_of(own_keys[1], (LEV, NX, NY), ((1, 16),), -0.2, 0.2), 0.0, 1.0).astype(jnp.bfloat16)
    frac_y = jnp.clip(1.0 * jax.random.uniform(own_keys[2], (LEV, NX, NY), jnp.float32) ** steps_of(own_keys[2], (LEV, NX, NY), ((1, 16),), -0.2, 0.2), 0.0, 1.0).astype(jnp.bfloat16)
    vertical_modes = bell_draw(key_list[3], (LEV, LEV), LEV ** -0.5, 0.875, (), jnp.float32)
    mode_projection = bell_draw(key_list[4], (LEV, LEV), LEV ** -0.5, 0.875, (), jnp.float32)
    mode_rates = jnp.clip(jnp.exp(jax.random.uniform(key_list[5], (LEV,), jnp.float32, math.log(1.0), math.log(40.0))), 1.0, 40.0)
    return dict(tracer=tracer, frac_x=frac_x, frac_y=frac_y, vertical_modes=vertical_modes, mode_projection=mode_projection, mode_rates=mode_rates)


def lagrange_weights(fraction):
    position = 1.0 - fraction.astype(jnp.float32)
    return (
        -position * (position - 1.0) * (position - 2.0) / 6.0,
        (position + 1.0) * (position - 1.0) * (position - 2.0) / 2.0,
        -(position + 1.0) * position * (position - 2.0) / 2.0,
        (position + 1.0) * position * (position - 1.0) / 6.0,
    )


def drift_classes(levels):
    bounds = []
    for category in range(9):
        first_level = (category * levels + 8) // 9
        last_level = ((category + 1) * levels + 8) // 9
        bounds.append((first_level, last_level, category - 4))
    return bounds


def sweep(values, fraction, axis_number):
    weights = lagrange_weights(fraction)
    pieces_out = []
    for first_level, last_level, displace in drift_classes(values.shape[0]):
        section = values[first_level:last_level]
        summed = jnp.zeros(section.shape, jnp.float32)
        for stencil in range(4):
            offset = stencil - 2 - displace
            summed = summed + weights[stencil][first_level:last_level] * jnp.roll(section, -offset, axis=axis_number)
        pieces_out.append(summed)
    return jnp.concatenate(pieces_out, axis=0)


def reference(tracer, frac_x, frac_y, vertical_modes, mode_projection, mode_rates):
    interim = sweep(tracer, frac_y, 2)
    advected = sweep(interim, frac_x, 1)
    spectrum = jnp.fft.fft(jnp.fft.rfft(advected, axis=2)[:, :, :KY], axis=1)
    kept_modes = jnp.concatenate([jnp.arange(KX // 2, dtype=jnp.int32), jnp.arange(NX - KX // 2, NX, dtype=jnp.int32)])
    spectrum = spectrum[:, kept_modes, :]
    index_x = jnp.arange(KX, dtype=jnp.int32)
    wave_x = jnp.where(index_x < KX // 2, index_x, index_x - KX).astype(jnp.float32)
    wave_y = jnp.arange(KY, dtype=jnp.int32).astype(jnp.float32)
    kappa = ((2.0 * wave_x / NX) ** 2)[:, None] + ((2.0 * wave_y / NY) ** 2)[None, :]
    factor = 1.0 / (1.0 + mode_rates[:, None, None] * kappa[None])

    def solve_part(component):
        projected = jnp.einsum("al,lmk->amk", mode_projection, component, precision=lax.Precision.HIGHEST)
        return jnp.einsum("la,amk->lmk", vertical_modes, projected * factor, precision=lax.Precision.HIGHEST)

    solved = solve_part(jnp.real(spectrum)) + 1j * solve_part(jnp.imag(spectrum))
    spread_out = jnp.zeros((LEV, NX, KY), solved.dtype).at[:, kept_modes, :].set(solved)
    return jnp.fft.irfft(jnp.fft.ifft(spread_out, axis=1), n=NY, axis=2).astype(jnp.float32)
```

```python
import math

import jax
import jax.numpy as jnp
import ml_dtypes
import numpy as np
from jax import lax
from jax.experimental import pallas as pl
from jax.experimental.pallas import tpu as pltpu
from jax.sharding import PartitionSpec as P

HALO = 6


def padded_2(value, sides, width):
    for axis, dim in sides:
        size, length = (lax.axis_size(axis), value.shape[dim])
        up = [(i, (i + 1) % size) for i in range(size)]
        down = [(j, i) for i, j in up]
        last = lax.slice_in_dim(value, length - width, length, axis=dim)
        initial = lax.slice_in_dim(value, 0, width, axis=dim)
        before = lax.ppermute(last, axis, up)
        after = lax.ppermute(initial, axis, down)
        value = jnp.concatenate([before, value, after], axis=dim)
    return value


def lagrange_weights(fraction):
    position = 1.0 - fraction.astype(jnp.float32)
    return (
        -position * (position - 1.0) * (position - 2.0) / 6.0,
        (position + 1.0) * (position - 1.0) * (position - 2.0) / 2.0,
        -(position + 1.0) * position * (position - 2.0) / 2.0,
        (position + 1.0) * position * (position - 1.0) / 6.0,
    )


def drift_classes(levels):
    bounds = []
    for category in range(9):
        first_level = (category * levels + 8) // 9
        last_level = ((category + 1) * levels + 8) // 9
        bounds.append((first_level, last_level, category - 4))
    return bounds


def sweep_columns(values, fraction):
    weights = lagrange_weights(fraction)
    pieces_out = []
    for first_level, last_level, displace in drift_classes(values.shape[0]):
        section = values[first_level:last_level]
        summed = jnp.zeros(section.shape, jnp.float32)
        for stencil in range(4):
            offset = stencil - 2 - displace
            summed = summed + weights[stencil][first_level:last_level] * jnp.roll(
                section, -offset, axis=2
            )
        pieces_out.append(summed)
    return jnp.concatenate(pieces_out, axis=0)


def blend_rows(window, weights, first_level, last_level, displace, anchor, rows_here):
    summed = jnp.zeros((last_level - first_level, rows_here, window.shape[2]), jnp.float32)
    for stencil in range(4):
        offset = anchor + stencil - 2 - displace
        summed = (
            summed
            + weights[stencil][first_level:last_level] * window[:, offset : offset + rows_here]
        )
    return summed


def phase_angles(numbers, places, length):
    phases = jnp.mod(numbers[:, None] * places[None, :], length)
    return phases.astype(jnp.float32) * (2.0 * math.pi / length)


def plain_body(tracer, frac_x, frac_y, vertical_modes, mode_projection, mode_rates):
    levels, rows_here, columns = tracer.shape
    shards = lax.axis_size("gx")
    length_x = rows_here * shards
    modes_x = length_x // 2
    modes_y = columns // 2
    modes_here = modes_y // shards
    interim = sweep_columns(tracer, frac_y)
    weights = lagrange_weights(frac_x)
    classes = drift_classes(levels)
    pieces_out = []
    padded = padded_2(interim, (("gx", 1),), HALO)
    for first_level, last_level, displace in classes:
        pieces_out.append(
            blend_rows(
                padded[first_level:last_level],
                weights,
                first_level,
                last_level,
                displace,
                HALO,
                rows_here,
            )
        )
    advected = jnp.concatenate(pieces_out, axis=0)
    wave_y = jnp.arange(modes_y, dtype=jnp.int32)
    angle_y = phase_angles(wave_y, jnp.arange(columns, dtype=jnp.int32), columns)
    table_y = jnp.stack([jnp.cos(angle_y), -jnp.sin(angle_y)], axis=1).reshape(2 * modes_y, columns)
    flattened = advected.reshape(levels * rows_here, columns)
    coefficients = lax.dot_general(
        table_y, flattened, (((1,), (1,)), ((), ())), precision=lax.Precision.HIGHEST
    )
    coefficients = coefficients.reshape(shards, modes_here, 2, levels * rows_here)
    wave_square = ((2.0 * wave_y.astype(jnp.float32) / columns) ** 2).reshape(shards, modes_here, 1)
    index_x = jnp.arange(modes_x, dtype=jnp.int32)
    wave_x = jnp.where(index_x < modes_x // 2, index_x, index_x - modes_x)
    angle_x = phase_angles(wave_x, jnp.arange(length_x, dtype=jnp.int32), length_x)
    cosine = jnp.cos(angle_x)
    sine = jnp.sin(angle_x)
    forward_x = jnp.stack(
        [jnp.stack([cosine.T, -sine.T], axis=1), jnp.stack([sine.T, cosine.T], axis=1)], axis=1
    )
    forward_x = forward_x.reshape(shards, rows_here, 2, 2, modes_x)
    inverse_x = (
        jnp.stack([jnp.stack([cosine, sine], axis=-1), jnp.stack([-sine, cosine], axis=-1)], axis=0)
        / length_x
    )
    inverse_x = inverse_x.reshape(2, modes_x, shards, rows_here, 2)
    square_x = (2.0 * wave_x.astype(jnp.float32) / length_x) ** 2
    spectral_in = lax.all_to_all(coefficients, "gx", split_axis=0, concat_axis=0, tiled=True)
    square_in = lax.all_to_all(wave_square, "gx", split_axis=0, concat_axis=0, tiled=True)
    item_count = spectral_in.shape[1]
    blocks = spectral_in.reshape(shards, item_count, 2, levels, rows_here)
    spectra = jnp.einsum("nkplc,ncpqm->kqlm", blocks, forward_x, precision=lax.Precision.HIGHEST)
    projected = jnp.einsum(
        "al,kqlm->kqam", mode_projection, spectra, precision=lax.Precision.HIGHEST
    )
    kappa = square_in[0][:, :, None] + square_x[None, None, :]
    factor = 1.0 / (1.0 + mode_rates[None, :, None] * kappa)
    solved = jnp.einsum(
        "la,kqam->kqlm",
        vertical_modes,
        projected * factor[:, None],
        precision=lax.Precision.HIGHEST,
    )
    returned = jnp.einsum("kqlm,qmncp->nkplc", solved, inverse_x, precision=lax.Precision.HIGHEST)
    returned = returned.reshape(shards, item_count, 2, levels * rows_here)
    merged = lax.all_to_all(returned, "gx", split_axis=0, concat_axis=0, tiled=True)
    weights_y = jnp.where(wave_y == 0, 1.0, 2.0).astype(jnp.float32) / columns
    table_back = table_y * jnp.repeat(weights_y, 2)[:, None]
    updated = lax.dot_general(
        merged.reshape(2 * modes_y, levels * rows_here),
        table_back,
        (((0,), (0,)), ((), ())),
        precision=lax.Precision.HIGHEST,
    )
    return updated.reshape(levels, rows_here, columns)


CHUNK = 16
GROUP = 8
VMEM_BYTES = 56 * 1024 * 1024
BF16 = jnp.bfloat16
F32 = jnp.float32


def drift_of(level, levels):
    return (9 * level) // levels - 4


def group_drifts(group, levels):
    first = drift_of(GROUP * group, levels)
    last = drift_of(GROUP * group + GROUP - 1, levels)
    split = next(
        (s for s in range(GROUP) if drift_of(GROUP * group + s, levels) != first), GROUP
    )
    return first, last, split


def halo_groups(levels, rows_here):
    before, after = [], []
    for j in range(rows_here + 3):
        for group in range(levels // GROUP):
            first, last, _ = group_drifts(group, levels)
            if j - 2 - last < 0:
                before.append((j, group))
            if j - 2 - first >= rows_here:
                after.append((j, group))
    return before, after


def split_two(value):
    high = value.astype(BF16)
    return high, (value - high.astype(F32)).astype(BF16)


def dot3(left, right, dims):
    def dot(a, b):
        return lax.dot_general(a, b, (dims, ((), ())), preferred_element_type=F32)

    return dot(left[0], right[0]) + (dot(left[0], right[1]) + dot(left[1], right[0]))


def kernel_weights(fraction):
    p = 1.0 - fraction
    low, lower, upper = p - 1.0, p - 2.0, p + 1.0
    a, b = p * low, upper * lower
    return (
        a * lower * (-1.0 / 6.0),
        b * low * 0.5,
        b * p * (-0.5),
        a * upper * (1.0 / 6.0),
    )


def upper_mask(split, width):
    return lax.broadcasted_iota(jnp.int32, (GROUP, width), 0) >= split


def y_sweep_kernel(tracer, frac, interim, before_out, after_out):
    rows_here, levels, columns = tracer.shape
    for pair in range(levels // (2 * GROUP)):

        @pl.loop(0, rows_here)
        def _(i, pair=pair):
            fractions = frac[i, 2 * GROUP * pair : 2 * GROUP * (pair + 1), :].astype(F32)
            for half in range(2):
                group = 2 * pair + half
                first, last, split = group_drifts(group, levels)
                weights = kernel_weights(fractions[GROUP * half : GROUP * (half + 1)])
                value = tracer[i, GROUP * group : GROUP * (group + 1), :]
                rolled = [
                    pltpu.roll(value, (-(t - 2 - last)) % columns, 1)
                    for t in range(4 + last - first)
                ]
                mask = upper_mask(split, columns)
                total = None
                for tap in range(4):
                    source = rolled[tap]
                    if last != first:
                        source = jnp.where(mask, rolled[tap], rolled[tap + 1])
                    term = weights[tap] * source
                    total = term if total is None else total + term
                interim[i, GROUP * group : GROUP * (group + 1), :] = total

    before, after = halo_groups(levels, rows_here)
    for out, blocks, shift in ((before_out, before, rows_here), (after_out, after, -rows_here)):
        for at, (j, group) in enumerate(blocks):
            first, last, split = group_drifts(group, levels)
            picks = []
            for drift in (first, last):
                row = min(max(j - 2 - drift + shift, 0), rows_here - 1)
                picks.append(interim[row, GROUP * group : GROUP * (group + 1), :])
            out[GROUP * at : GROUP * (at + 1), :] = jnp.where(
                upper_mask(split, picks[0].shape[1]), picks[1], picks[0]
            )


def x_sweep_kernel(interim, frac, before_in, after_in, high_out, low_out):
    rows_here, levels, columns = interim.shape
    before, after = halo_groups(levels, rows_here)
    width = 256

    for pair in range(levels // (2 * GROUP)):

        @pl.loop(0, columns // width)
        def _(step, pair=pair):
            lanes = pl.ds(pl.multiple_of(step * width, width), width)
            windows = []
            for group in (2 * pair, 2 * pair + 1):
                first, last, split = group_drifts(group, levels)
                mask = upper_mask(split, width)
                window = []
                for j in range(rows_here + 3):
                    picks = []
                    for drift in (first, last):
                        row = j - 2 - drift
                        if row < 0:
                            at = GROUP * before.index((j, group))
                            picks.append(before_in[at : at + GROUP, lanes])
                        elif row >= rows_here:
                            at = GROUP * after.index((j, group))
                            picks.append(after_in[at : at + GROUP, lanes])
                        else:
                            at = GROUP * group
                            picks.append(interim[row, at : at + GROUP, lanes])
                    window.append(jnp.where(mask, picks[1], picks[0]))
                windows.append(window)
            for i in range(rows_here):
                at = 2 * GROUP * pair
                weights = kernel_weights(frac[i, at : at + 2 * GROUP, lanes].astype(F32))
                parts = []
                for half in range(2):
                    total = None
                    for tap in range(4):
                        term = (
                            weights[tap][GROUP * half : GROUP * (half + 1)]
                            * windows[half][i + tap]
                        )
                        total = term if total is None else total + term
                    parts.append(total)
                high, low = split_two(jnp.concatenate(parts, axis=0))
                high_out[levels * i + at : levels * i + at + 2 * GROUP, lanes] = high
                low_out[levels * i + at : levels * i + at + 2 * GROUP, lanes] = low


def pack_block(block):
    return jnp.concatenate([block[8 * g : 8 * g + 8] for g in range(4)], axis=1)


def unpack_block(block):
    width = block.shape[1] // 4
    return jnp.concatenate([block[:, width * g : width * (g + 1)] for g in range(4)], axis=0)


def forward_kernel(high, low, table_high, table_low, out):
    shards = out.shape[0]
    rows = table_high.shape[0] // 2
    for part in range(2):
        span = slice(part * rows, (part + 1) * rows)
        result = dot3(
            (table_high[span], table_low[span]), (high[...], low[...]), ((1,), (1,))
        )
        for n in range(shards // 2):
            out[part * (shards // 2) + n] = pack_block(result[32 * n : 32 * n + 32])


def solve_kernel(
    blocks, f_high, f_low, g_high, g_low, twiddle_re, twiddle_im, project, back, kappa, rates, out
):
    shards = blocks.shape[0]
    data = jnp.concatenate([unpack_block(blocks[n]) for n in range(shards)], axis=0)
    plain = ((1,), (0,))
    mixed = dot3((f_high[...], f_low[...]), split_two(data), plain)
    half = mixed.shape[0] // 2
    real, imag = mixed[:half], mixed[half:]
    project_two = split_two(project[...])
    rate = rates[...]
    scale = kappa[:, 3:4]
    out_re = out_im = None
    for part in range(3):
        t_re, t_im = twiddle_re[part], twiddle_im[part]
        turned = (real * t_re - imag * t_im, real * t_im + imag * t_re)
        factor = scale / (1.0 + rate * kappa[:, part : part + 1])
        y_re, y_im = (dot3(split_two(u), project_two, plain) * factor for u in turned)
        a_re = y_re * t_re + y_im * t_im
        a_im = y_im * t_re - y_re * t_im
        out_re = a_re if part == 0 else out_re + a_re
        out_im = a_im if part == 0 else out_im + a_im
    back_two = split_two(back[...])
    solved = jnp.concatenate(
        [dot3(split_two(u), back_two, plain) for u in (out_re, out_im)], axis=0
    )
    result = dot3((g_high[...], g_low[...]), split_two(solved), plain)
    for n in range(shards):
        out[n] = pack_block(result[32 * n : 32 * n + 32])


def inverse_kernel(blocks, table_high, table_low, *rest):
    out = rest[-1]
    data = jnp.concatenate([unpack_block(blocks[n]) for n in range(blocks.shape[0])], axis=0)
    high, low = split_two(data.T)
    width = 512
    for step in range(out.shape[1] // width):
        lanes = slice(step * width, (step + 1) * width)
        value = dot3((high, low), (table_high[:, lanes], table_low[:, lanes]), ((1,), (0,)))
        out[:, lanes] = value if len(rest) == 1 else value + rest[0][:, lanes]


def call(kernel, shapes, flops, args, aliases=None):
    size = sum(math.prod(a.shape) * a.dtype.itemsize for a in (*args, *shapes))
    return pl.pallas_call(
        kernel,
        out_shape=shapes,
        in_specs=[pl.BlockSpec(memory_space=pltpu.VMEM)] * len(args),
        out_specs=[pl.BlockSpec(memory_space=pltpu.VMEM)] * len(shapes),
        input_output_aliases=aliases or {},
        compiler_params=pltpu.CompilerParams(vmem_limit_bytes=VMEM_BYTES),
        cost_estimate=pl.CostEstimate(flops=flops, bytes_accessed=size, transcendentals=0),
    )(*args)


def two_parts(table):
    high = table.astype(ml_dtypes.bfloat16)
    low = (table - high.astype(np.float64)).astype(ml_dtypes.bfloat16)
    return high, low


def y_table(columns, shards, modes_here):
    wave = np.arange(shards * modes_here).reshape(shards, modes_here // CHUNK, CHUNK)
    wave = wave.transpose(1, 0, 2)[..., None]
    angle = (wave * np.arange(columns) % columns) * (2.0 * np.pi / columns)
    table = np.stack([np.cos(angle), -np.sin(angle)], axis=3)
    return two_parts(table.reshape(modes_here // CHUNK, shards * CHUNK * 2, columns))


def x_tables(shards, rows_here, levels):
    n = np.arange(shards)
    angle = (n[:, None] * n[None, :] % shards) * (2.0 * np.pi / shards)
    c, s = np.cos(angle), np.sin(angle)
    forward = np.stack([np.stack([c, s], 1), np.stack([-s, c], 1)], 0)
    eye = np.eye(CHUNK)
    size = 2 * shards * CHUNK
    forward = np.einsum("pmqn,kj->pmknjq", forward, eye).reshape(size, size)
    length_x = shards * rows_here
    modes_x = length_x // 2
    m = np.arange(modes_x)
    wave = np.where(m < modes_x // 2, m, m - modes_x)
    turn = (wave[:, None] * np.arange(rows_here) % length_x) * (2.0 * np.pi / length_x)
    turn = turn.reshape(-1, shards, 1, rows_here, 1)
    shape = (turn.shape[0], shards, CHUNK, rows_here, levels)
    turn = np.broadcast_to(turn, shape).reshape(-1, shards * CHUNK, rows_here * levels)
    square = ((2.0 * wave / length_x) ** 2).reshape(-1, shards).T
    square = np.repeat(square, CHUNK, axis=0).astype(np.float32)
    return (
        two_parts(forward),
        two_parts(np.ascontiguousarray(forward.T)),
        np.cos(turn).astype(np.float32),
        (-np.sin(turn)).astype(np.float32),
        square,
    )


def body(tracer, frac_x, frac_y, vertical_modes, mode_projection, mode_rates):
    levels, rows_here, columns = tracer.shape
    shards = lax.axis_size("gx")
    length_x = rows_here * shards
    modes_y = columns // 2
    modes_here = modes_y // shards
    fits = (
        shards == 16
        and modes_here % CHUNK == 0
        and length_x // 2 == 3 * shards
        and levels % (2 * GROUP) == 0
        and levels <= 48
        and columns % 512 == 0
        and all(
            group_drifts(g, levels)[1] - group_drifts(g, levels)[0] == 1
            for g in range(levels // GROUP)
        )
    )
    if not fits:
        return plain_body(tracer, frac_x, frac_y, vertical_modes, mode_projection, mode_rates)
    lines = rows_here * levels
    chunks = modes_here // CHUNK
    before, after = halo_groups(levels, rows_here)
    interim, to_right, to_left = call(
        y_sweep_kernel,
        [
            jax.ShapeDtypeStruct((rows_here, levels, columns), F32),
            jax.ShapeDtypeStruct((GROUP * len(before), columns), F32),
            jax.ShapeDtypeStruct((GROUP * len(after), columns), F32),
        ],
        40 * lines * columns,
        (jnp.swapaxes(tracer, 0, 1), jnp.swapaxes(frac_y, 0, 1)),
    )
    up = [(i, (i + 1) % shards) for i in range(shards)]
    from_left = lax.ppermute(to_right, "gx", up)
    from_right = lax.ppermute(to_left, "gx", [(j, i) for i, j in up])
    high, low = call(
        x_sweep_kernel,
        [jax.ShapeDtypeStruct((lines, columns), BF16)] * 2,
        40 * lines * columns,
        (interim, jnp.swapaxes(frac_x, 0, 1), from_left, from_right),
    )

    t_high, t_low = y_table(columns, shards, modes_here)
    f_two, g_two, twiddle_re, twiddle_im, square_x = x_tables(shards, rows_here, levels)
    eye = jnp.eye(rows_here, dtype=F32)
    project = jnp.tile(mode_projection.T, (rows_here, rows_here))
    back = (eye[:, None, :, None] * vertical_modes.T[None, :, None, :]).reshape(lines, lines)
    rates = jnp.tile(mode_rates, rows_here)[None, :]
    size = shards * CHUNK * 2
    block = jax.ShapeDtypeStruct((shards, 8, 4 * lines), F32)

    kappas, tables = [], []
    for c in range(chunks):
        wave = lax.axis_index("gx") * modes_here + c * CHUNK + jnp.arange(CHUNK, dtype=jnp.int32)
        square_y = jnp.tile((2.0 * wave.astype(F32) / columns) ** 2, shards)[:, None]
        scale = jnp.where(wave == 0, 1.0, 2.0).astype(F32) / (columns * length_x)
        kappas.append(
            jnp.concatenate([square_x + square_y, jnp.tile(scale, shards)[:, None]], axis=1)
        )
        tables.append((jnp.asarray(t_high[c]), jnp.asarray(t_low[c])))

    def swap(value):
        return lax.all_to_all(value, "gx", split_axis=0, concat_axis=0, tiled=True)

    received = []
    for c in range(chunks):
        (sent,) = call(
            forward_kernel, [block], 6 * size * columns * lines, (high, low, *tables[c])
        )
        received.append(swap(sent))
    returned = []
    for c in range(chunks):
        (solved,) = call(
            solve_kernel,
            [block],
            12 * size * size * lines + 24 * size * lines * lines,
            (
                received[c],
                *map(jnp.asarray, (*f_two, *g_two, twiddle_re, twiddle_im)),
                project,
                back,
                kappas[c],
                rates,
            ),
        )
        returned.append(swap(solved))
    total = ()
    for c in range(chunks):
        total = call(
            inverse_kernel,
            [jax.ShapeDtypeStruct((lines, columns), F32)],
            6 * size * columns * lines,
            (returned[c], *tables[c], *total),
            {3: 0} if c else None,
        )
    return jnp.swapaxes(total[0].reshape(rows_here, levels, columns), 0, 1)


def solution(mesh):
    placed = (
        P("member", "gx", None),
        P("member", "gx", None),
        P("member", "gx", None),
        P(),
        P(),
        P(),
    )
    return jax.shard_map(
        body, mesh=mesh, in_specs=placed, out_specs=P("member", "gx", None), check_vma=False
    )
```

```python
import math

import jax
import jax.numpy as jnp
import ml_dtypes
import numpy as np
from jax import lax
from jax.experimental import pallas as pl
from jax.experimental.pallas import tpu as pltpu
from jax.sharding import PartitionSpec as P

HALO = 6


def padded_2(value, sides, width):
    for axis, dim in sides:
        size, length = (lax.axis_size(axis), value.shape[dim])
        up = [(i, (i + 1) % size) for i in range(size)]
        down = [(j, i) for i, j in up]
        last = lax.slice_in_dim(value, length - width, length, axis=dim)
        initial = lax.slice_in_dim(value, 0, width, axis=dim)
        before = lax.ppermute(last, axis, up)
        after = lax.ppermute(initial, axis, down)
        value = jnp.concatenate([before, value, after], axis=dim)
    return value


def lagrange_weights(fraction):
    position = 1.0 - fraction.astype(jnp.float32)
    return (
        -position * (position - 1.0) * (position - 2.0) / 6.0,
        (position + 1.0) * (position - 1.0) * (position - 2.0) / 2.0,
        -(position + 1.0) * position * (position - 2.0) / 2.0,
        (position + 1.0) * position * (position - 1.0) / 6.0,
    )


def drift_classes(levels):
    bounds = []
    for category in range(9):
        first_level = (category * levels + 8) // 9
        last_level = ((category + 1) * levels + 8) // 9
        bounds.append((first_level, last_level, category - 4))
    return bounds


def sweep_columns(values, fraction):
    weights = lagrange_weights(fraction)
    pieces_out = []
    for first_level, last_level, displace in drift_classes(values.shape[0]):
        section = values[first_level:last_level]
        summed = jnp.zeros(section.shape, jnp.float32)
        for stencil in range(4):
            offset = stencil - 2 - displace
            summed = summed + weights[stencil][first_level:last_level] * jnp.roll(
                section, -offset, axis=2
            )
        pieces_out.append(summed)
    return jnp.concatenate(pieces_out, axis=0)


def blend_rows(window, weights, first_level, last_level, displace, anchor, rows_here):
    summed = jnp.zeros((last_level - first_level, rows_here, window.shape[2]), jnp.float32)
    for stencil in range(4):
        offset = anchor + stencil - 2 - displace
        summed = (
            summed
            + weights[stencil][first_level:last_level] * window[:, offset : offset + rows_here]
        )
    return summed


def phase_angles(numbers, places, length):
    phases = jnp.mod(numbers[:, None] * places[None, :], length)
    return phases.astype(jnp.float32) * (2.0 * math.pi / length)


def plain_body(tracer, frac_x, frac_y, vertical_modes, mode_projection, mode_rates):
    levels, rows_here, columns = tracer.shape
    shards = lax.axis_size("gx")
    length_x = rows_here * shards
    modes_x = length_x // 2
    modes_y = columns // 2
    modes_here = modes_y // shards
    interim = sweep_columns(tracer, frac_y)
    weights = lagrange_weights(frac_x)
    classes = drift_classes(levels)
    pieces_out = []
    padded = padded_2(interim, (("gx", 1),), HALO)
    for first_level, last_level, displace in classes:
        pieces_out.append(
            blend_rows(
                padded[first_level:last_level],
                weights,
                first_level,
                last_level,
                displace,
                HALO,
                rows_here,
            )
        )
    advected = jnp.concatenate(pieces_out, axis=0)
    wave_y = jnp.arange(modes_y, dtype=jnp.int32)
    angle_y = phase_angles(wave_y, jnp.arange(columns, dtype=jnp.int32), columns)
    table_y = jnp.stack([jnp.cos(angle_y), -jnp.sin(angle_y)], axis=1).reshape(2 * modes_y, columns)
    flattened = advected.reshape(levels * rows_here, columns)
    coefficients = lax.dot_general(
        table_y, flattened, (((1,), (1,)), ((), ())), precision=lax.Precision.HIGHEST
    )
    coefficients = coefficients.reshape(shards, modes_here, 2, levels * rows_here)
    wave_square = ((2.0 * wave_y.astype(jnp.float32) / columns) ** 2).reshape(shards, modes_here, 1)
    index_x = jnp.arange(modes_x, dtype=jnp.int32)
    wave_x = jnp.where(index_x < modes_x // 2, index_x, index_x - modes_x)
    angle_x = phase_angles(wave_x, jnp.arange(length_x, dtype=jnp.int32), length_x)
    cosine = jnp.cos(angle_x)
    sine = jnp.sin(angle_x)
    forward_x = jnp.stack(
        [jnp.stack([cosine.T, -sine.T], axis=1), jnp.stack([sine.T, cosine.T], axis=1)], axis=1
    )
    forward_x = forward_x.reshape(shards, rows_here, 2, 2, modes_x)
    inverse_x = (
        jnp.stack([jnp.stack([cosine, sine], axis=-1), jnp.stack([-sine, cosine], axis=-1)], axis=0)
        / length_x
    )
    inverse_x = inverse_x.reshape(2, modes_x, shards, rows_here, 2)
    square_x = (2.0 * wave_x.astype(jnp.float32) / length_x) ** 2
    spectral_in = lax.all_to_all(coefficients, "gx", split_axis=0, concat_axis=0, tiled=True)
    square_in = lax.all_to_all(wave_square, "gx", split_axis=0, concat_axis=0, tiled=True)
    item_count = spectral_in.shape[1]
    blocks = spectral_in.reshape(shards, item_count, 2, levels, rows_here)
    spectra = jnp.einsum("nkplc,ncpqm->kqlm", blocks, forward_x, precision=lax.Precision.HIGHEST)
    projected = jnp.einsum(
        "al,kqlm->kqam", mode_projection, spectra, precision=lax.Precision.HIGHEST
    )
    kappa = square_in[0][:, :, None] + square_x[None, None, :]
    factor = 1.0 / (1.0 + mode_rates[None, :, None] * kappa)
    solved = jnp.einsum(
        "la,kqam->kqlm",
        vertical_modes,
        projected * factor[:, None],
        precision=lax.Precision.HIGHEST,
    )
    returned = jnp.einsum("kqlm,qmncp->nkplc", solved, inverse_x, precision=lax.Precision.HIGHEST)
    returned = returned.reshape(shards, item_count, 2, levels * rows_here)
    merged = lax.all_to_all(returned, "gx", split_axis=0, concat_axis=0, tiled=True)
    weights_y = jnp.where(wave_y == 0, 1.0, 2.0).astype(jnp.float32) / columns
    table_back = table_y * jnp.repeat(weights_y, 2)[:, None]
    updated = lax.dot_general(
        merged.reshape(2 * modes_y, levels * rows_here),
        table_back,
        (((0,), (0,)), ((), ())),
        precision=lax.Precision.HIGHEST,
    )
    return updated.reshape(levels, rows_here, columns)


CHUNK = 24
GROUP = 8
SPAN = 2 * CHUNK
PIECES = SPAN // 8
VMEM_BYTES = 56 * 1024 * 1024
BF16 = jnp.bfloat16
F32 = jnp.float32


def drift_of(level, levels):
    return (9 * level) // levels - 4


def group_drifts(group, levels):
    first = drift_of(GROUP * group, levels)
    last = drift_of(GROUP * group + GROUP - 1, levels)
    split = next(
        (s for s in range(GROUP) if drift_of(GROUP * group + s, levels) != first), GROUP
    )
    return first, last, split


def halo_groups(levels, rows_here):
    before, after = [], []
    for j in range(rows_here + 3):
        for group in range(levels // GROUP):
            first, last, _ = group_drifts(group, levels)
            if j - 2 - last < 0:
                before.append((j, group))
            if j - 2 - first >= rows_here:
                after.append((j, group))
    return before, after


def split_two(value):
    high = value.astype(BF16)
    return high, (value - high.astype(F32)).astype(BF16)


def dot3(left, right, dims):
    def dot(a, b):
        return lax.dot_general(a, b, (dims, ((), ())), preferred_element_type=F32)

    return dot(left[0], right[0]) + (dot(left[0], right[1]) + dot(left[1], right[0]))


def kernel_weights(fraction):
    p = 1.0 - fraction
    low, lower, upper = p - 1.0, p - 2.0, p + 1.0
    a, b = p * low, upper * lower
    return (
        a * lower * (-1.0 / 6.0),
        b * low * 0.5,
        b * p * (-0.5),
        a * upper * (1.0 / 6.0),
    )


def upper_mask(split, width):
    return lax.broadcasted_iota(jnp.int32, (GROUP, width), 0) >= split


def y_sweep_kernel(tracer, frac, interim, before_out, after_out):
    rows_here, levels, columns = tracer.shape
    for pair in range(levels // (2 * GROUP)):

        @pl.loop(0, rows_here)
        def _(i, pair=pair):
            fractions = frac[i, 2 * GROUP * pair : 2 * GROUP * (pair + 1), :].astype(F32)
            for half in range(2):
                group = 2 * pair + half
                first, last, split = group_drifts(group, levels)
                weights = kernel_weights(fractions[GROUP * half : GROUP * (half + 1)])
                value = tracer[i, GROUP * group : GROUP * (group + 1), :]
                rolled = [
                    pltpu.roll(value, (-(t - 2 - last)) % columns, 1)
                    for t in range(4 + last - first)
                ]
                mask = upper_mask(split, columns)
                total = None
                for tap in range(4):
                    source = rolled[tap]
                    if last != first:
                        source = jnp.where(mask, rolled[tap], rolled[tap + 1])
                    term = weights[tap] * source
                    total = term if total is None else total + term
                interim[i, GROUP * group : GROUP * (group + 1), :] = total

    before, after = halo_groups(levels, rows_here)
    for out, blocks, shift in ((before_out, before, rows_here), (after_out, after, -rows_here)):
        for at, (j, group) in enumerate(blocks):
            first, last, split = group_drifts(group, levels)
            picks = []
            for drift in (first, last):
                row = min(max(j - 2 - drift + shift, 0), rows_here - 1)
                picks.append(interim[row, GROUP * group : GROUP * (group + 1), :])
            out[GROUP * at : GROUP * (at + 1), :] = jnp.where(
                upper_mask(split, picks[0].shape[1]), picks[1], picks[0]
            )


def x_sweep_kernel(interim, frac, before_in, after_in, high_out, low_out):
    rows_here, levels, columns = interim.shape
    before, after = halo_groups(levels, rows_here)
    width = 256

    for pair in range(levels // (2 * GROUP)):

        @pl.loop(0, columns // width)
        def _(step, pair=pair):
            lanes = pl.ds(pl.multiple_of(step * width, width), width)
            windows = []
            for group in (2 * pair, 2 * pair + 1):
                first, last, split = group_drifts(group, levels)
                mask = upper_mask(split, width)
                window = []
                for j in range(rows_here + 3):
                    picks = []
                    for drift in (first, last):
                        row = j - 2 - drift
                        if row < 0:
                            at = GROUP * before.index((j, group))
                            picks.append(before_in[at : at + GROUP, lanes])
                        elif row >= rows_here:
                            at = GROUP * after.index((j, group))
                            picks.append(after_in[at : at + GROUP, lanes])
                        else:
                            at = GROUP * group
                            picks.append(interim[row, at : at + GROUP, lanes])
                    window.append(jnp.where(mask, picks[1], picks[0]))
                windows.append(window)
            for i in range(rows_here):
                at = 2 * GROUP * pair
                weights = kernel_weights(frac[i, at : at + 2 * GROUP, lanes].astype(F32))
                parts = []
                for half in range(2):
                    total = None
                    for tap in range(4):
                        term = (
                            weights[tap][GROUP * half : GROUP * (half + 1)]
                            * windows[half][i + tap]
                        )
                        total = term if total is None else total + term
                    parts.append(total)
                high, low = split_two(jnp.concatenate(parts, axis=0))
                high_out[levels * i + at : levels * i + at + 2 * GROUP, lanes] = high
                low_out[levels * i + at : levels * i + at + 2 * GROUP, lanes] = low


def pack_block(block):
    return jnp.concatenate([block[8 * g : 8 * g + 8] for g in range(PIECES)], axis=1)


def unpack_block(block):
    width = block.shape[1] // PIECES
    return jnp.concatenate([block[:, width * g : width * (g + 1)] for g in range(PIECES)], axis=0)


def forward_kernel(high, low, table_high, table_low, out):
    shards = out.shape[0]
    rows = table_high.shape[0] // 2
    for part in range(2):
        span = slice(part * rows, (part + 1) * rows)
        result = dot3(
            (table_high[span], table_low[span]), (high[...], low[...]), ((1,), (1,))
        )
        for n in range(shards // 2):
            out[part * (shards // 2) + n] = pack_block(result[SPAN * n : SPAN * n + SPAN])


def solve_kernel(
    blocks, f_high, f_low, g_high, g_low, twiddle_re, twiddle_im, project, back, kappa, rates, out
):
    shards = blocks.shape[0]
    data = jnp.concatenate([unpack_block(blocks[n]) for n in range(shards)], axis=0)
    plain = ((1,), (0,))
    mixed = dot3((f_high[...], f_low[...]), split_two(data), plain)
    half = mixed.shape[0] // 2
    real, imag = mixed[:half], mixed[half:]
    project_two = split_two(project[...])
    rate = rates[...]
    scale = kappa[:, 3:4]
    out_re = out_im = None
    for part in range(3):
        t_re, t_im = twiddle_re[part], twiddle_im[part]
        turned = (real * t_re - imag * t_im, real * t_im + imag * t_re)
        factor = scale / (1.0 + rate * kappa[:, part : part + 1])
        y_re, y_im = (dot3(split_two(u), project_two, plain) * factor for u in turned)
        a_re = y_re * t_re + y_im * t_im
        a_im = y_im * t_re - y_re * t_im
        out_re = a_re if part == 0 else out_re + a_re
        out_im = a_im if part == 0 else out_im + a_im
    back_two = split_two(back[...])
    solved = jnp.concatenate(
        [dot3(split_two(u), back_two, plain) for u in (out_re, out_im)], axis=0
    )
    result = dot3((g_high[...], g_low[...]), split_two(solved), plain)
    for n in range(shards):
        out[n] = pack_block(result[SPAN * n : SPAN * n + SPAN])


def inverse_kernel(blocks, table_high, table_low, *rest):
    out = rest[-1]
    data = jnp.concatenate([unpack_block(blocks[n]) for n in range(blocks.shape[0])], axis=0)
    high, low = split_two(data.T)
    width = 512
    for step in range(out.shape[1] // width):
        lanes = slice(step * width, (step + 1) * width)
        value = dot3((high, low), (table_high[:, lanes], table_low[:, lanes]), ((1,), (0,)))
        out[:, lanes] = value if len(rest) == 1 else value + rest[0][:, lanes]


def call(kernel, shapes, flops, args, aliases=None):
    size = sum(math.prod(a.shape) * a.dtype.itemsize for a in (*args, *shapes))
    return pl.pallas_call(
        kernel,
        out_shape=shapes,
        in_specs=[pl.BlockSpec(memory_space=pltpu.VMEM)] * len(args),
        out_specs=[pl.BlockSpec(memory_space=pltpu.VMEM)] * len(shapes),
        input_output_aliases=aliases or {},
        compiler_params=pltpu.CompilerParams(vmem_limit_bytes=VMEM_BYTES),
        cost_estimate=pl.CostEstimate(flops=flops, bytes_accessed=size, transcendentals=0),
    )(*args)


def two_parts(table):
    high = table.astype(ml_dtypes.bfloat16)
    low = (table - high.astype(np.float64)).astype(ml_dtypes.bfloat16)
    return high, low


def y_table(columns, shards, modes_here):
    wave = np.arange(shards * modes_here).reshape(shards, modes_here // CHUNK, CHUNK)
    wave = wave.transpose(1, 0, 2)[..., None]
    angle = (wave * np.arange(columns) % columns) * (2.0 * np.pi / columns)
    table = np.stack([np.cos(angle), -np.sin(angle)], axis=3)
    return two_parts(table.reshape(modes_here // CHUNK, shards * CHUNK * 2, columns))


def x_tables(shards, rows_here, levels):
    n = np.arange(shards)
    angle = (n[:, None] * n[None, :] % shards) * (2.0 * np.pi / shards)
    c, s = np.cos(angle), np.sin(angle)
    forward = np.stack([np.stack([c, s], 1), np.stack([-s, c], 1)], 0)
    eye = np.eye(CHUNK)
    size = 2 * shards * CHUNK
    forward = np.einsum("pmqn,kj->pmknjq", forward, eye).reshape(size, size)
    length_x = shards * rows_here
    modes_x = length_x // 2
    m = np.arange(modes_x)
    wave = np.where(m < modes_x // 2, m, m - modes_x)
    turn = (wave[:, None] * np.arange(rows_here) % length_x) * (2.0 * np.pi / length_x)
    turn = turn.reshape(-1, shards, 1, rows_here, 1)
    shape = (turn.shape[0], shards, CHUNK, rows_here, levels)
    turn = np.broadcast_to(turn, shape).reshape(-1, shards * CHUNK, rows_here * levels)
    square = ((2.0 * wave / length_x) ** 2).reshape(-1, shards).T
    square = np.repeat(square, CHUNK, axis=0).astype(np.float32)
    return (
        two_parts(forward),
        two_parts(np.ascontiguousarray(forward.T)),
        np.cos(turn).astype(np.float32),
        (-np.sin(turn)).astype(np.float32),
        square,
    )


def body(tracer, frac_x, frac_y, vertical_modes, mode_projection, mode_rates):
    levels, rows_here, columns = tracer.shape
    shards = lax.axis_size("gx")
    length_x = rows_here * shards
    modes_y = columns // 2
    modes_here = modes_y // shards
    fits = (
        shards == 16
        and modes_here % CHUNK == 0
        and length_x // 2 == 3 * shards
        and levels % (2 * GROUP) == 0
        and levels <= 48
        and columns % 512 == 0
        and all(
            group_drifts(g, levels)[1] - group_drifts(g, levels)[0] == 1
            for g in range(levels // GROUP)
        )
    )
    if not fits:
        return plain_body(tracer, frac_x, frac_y, vertical_modes, mode_projection, mode_rates)
    lines = rows_here * levels
    chunks = modes_here // CHUNK
    before, after = halo_groups(levels, rows_here)
    interim, to_right, to_left = call(
        y_sweep_kernel,
        [
            jax.ShapeDtypeStruct((rows_here, levels, columns), F32),
            jax.ShapeDtypeStruct((GROUP * len(before), columns), F32),
            jax.ShapeDtypeStruct((GROUP * len(after), columns), F32),
        ],
        40 * lines * columns,
        (jnp.swapaxes(tracer, 0, 1), jnp.swapaxes(frac_y, 0, 1)),
    )
    up = [(i, (i + 1) % shards) for i in range(shards)]
    from_left = lax.ppermute(to_right, "gx", up)
    from_right = lax.ppermute(to_left, "gx", [(j, i) for i, j in up])
    high, low = call(
        x_sweep_kernel,
        [jax.ShapeDtypeStruct((lines, columns), BF16)] * 2,
        40 * lines * columns,
        (interim, jnp.swapaxes(frac_x, 0, 1), from_left, from_right),
    )

    t_high, t_low = y_table(columns, shards, modes_here)
    f_two, g_two, twiddle_re, twiddle_im, square_x = x_tables(shards, rows_here, levels)
    eye = jnp.eye(rows_here, dtype=F32)
    project = jnp.tile(mode_projection.T, (rows_here, rows_here))
    back = (eye[:, None, :, None] * vertical_modes.T[None, :, None, :]).reshape(lines, lines)
    rates = jnp.tile(mode_rates, rows_here)[None, :]
    size = shards * CHUNK * 2
    block = jax.ShapeDtypeStruct((shards, 8, PIECES * lines), F32)

    kappas, tables = [], []
    for c in range(chunks):
        wave = lax.axis_index("gx") * modes_here + c * CHUNK + jnp.arange(CHUNK, dtype=jnp.int32)
        square_y = jnp.tile((2.0 * wave.astype(F32) / columns) ** 2, shards)[:, None]
        scale = jnp.where(wave == 0, 1.0, 2.0).astype(F32) / (columns * length_x)
        kappas.append(
            jnp.concatenate([square_x + square_y, jnp.tile(scale, shards)[:, None]], axis=1)
        )
        tables.append((jnp.asarray(t_high[c]), jnp.asarray(t_low[c])))

    def swap(value):
        return lax.all_to_all(value, "gx", split_axis=0, concat_axis=0, tiled=True)

    received = []
    for c in range(chunks):
        (sent,) = call(
            forward_kernel, [block], 6 * size * columns * lines, (high, low, *tables[c])
        )
        received.append(swap(sent))
    returned = []
    for c in range(chunks):
        (solved,) = call(
            solve_kernel,
            [block],
            12 * size * size * lines + 24 * size * lines * lines,
            (
                received[c],
                *map(jnp.asarray, (*f_two, *g_two, twiddle_re, twiddle_im)),
                project,
                back,
                kappas[c],
                rates,
            ),
        )
        returned.append(swap(solved))
    total = ()
    for c in range(chunks):
        total = call(
            inverse_kernel,
            [jax.ShapeDtypeStruct((lines, columns), F32)],
            6 * size * columns * lines,
            (returned[c], *tables[c], *total),
            {3: 0} if c else None,
        )
    return jnp.swapaxes(total[0].reshape(rows_here, levels, columns), 0, 1)


def solution(mesh):
    placed = (
        P("member", "gx", None),
        P("member", "gx", None),
        P("member", "gx", None),
        P(),
        P(),
        P(),
    )
    return jax.shard_map(
        body, mesh=mesh, in_specs=placed, out_specs=P("member", "gx", None), check_vma=False
    )
```

```python
import functools
import math

import jax
import jax.numpy as jnp
import ml_dtypes
import numpy as np
from jax import lax
from jax.experimental import pallas as pl
from jax.experimental.pallas import tpu as pltpu
from jax.sharding import PartitionSpec as P

HALO = 6


def padded_2(value, sides, width):
    for axis, dim in sides:
        size, length = (lax.axis_size(axis), value.shape[dim])
        up = [(i, (i + 1) % size) for i in range(size)]
        down = [(j, i) for i, j in up]
        last = lax.slice_in_dim(value, length - width, length, axis=dim)
        initial = lax.slice_in_dim(value, 0, width, axis=dim)
        before = lax.ppermute(last, axis, up)
        after = lax.ppermute(initial, axis, down)
        value = jnp.concatenate([before, value, after], axis=dim)
    return value


def lagrange_weights(fraction):
    position = 1.0 - fraction.astype(jnp.float32)
    return (
        -position * (position - 1.0) * (position - 2.0) / 6.0,
        (position + 1.0) * (position - 1.0) * (position - 2.0) / 2.0,
        -(position + 1.0) * position * (position - 2.0) / 2.0,
        (position + 1.0) * position * (position - 1.0) / 6.0,
    )


def drift_classes(levels):
    bounds = []
    for category in range(9):
        first_level = (category * levels + 8) // 9
        last_level = ((category + 1) * levels + 8) // 9
        bounds.append((first_level, last_level, category - 4))
    return bounds


def sweep_columns(values, fraction):
    weights = lagrange_weights(fraction)
    pieces_out = []
    for first_level, last_level, displace in drift_classes(values.shape[0]):
        section = values[first_level:last_level]
        summed = jnp.zeros(section.shape, jnp.float32)
        for stencil in range(4):
            offset = stencil - 2 - displace
            summed = summed + weights[stencil][first_level:last_level] * jnp.roll(
                section, -offset, axis=2
            )
        pieces_out.append(summed)
    return jnp.concatenate(pieces_out, axis=0)


def blend_rows(window, weights, first_level, last_level, displace, anchor, rows_here):
    summed = jnp.zeros((last_level - first_level, rows_here, window.shape[2]), jnp.float32)
    for stencil in range(4):
        offset = anchor + stencil - 2 - displace
        summed = (
            summed
            + weights[stencil][first_level:last_level] * window[:, offset : offset + rows_here]
        )
    return summed


def phase_angles(numbers, places, length):
    phases = jnp.mod(numbers[:, None] * places[None, :], length)
    return phases.astype(jnp.float32) * (2.0 * math.pi / length)


def plain_body(tracer, frac_x, frac_y, vertical_modes, mode_projection, mode_rates):
    levels, rows_here, columns = tracer.shape
    shards = lax.axis_size("gx")
    length_x = rows_here * shards
    modes_x = length_x // 2
    modes_y = columns // 2
    modes_here = modes_y // shards
    interim = sweep_columns(tracer, frac_y)
    weights = lagrange_weights(frac_x)
    classes = drift_classes(levels)
    pieces_out = []
    padded = padded_2(interim, (("gx", 1),), HALO)
    for first_level, last_level, displace in classes:
        pieces_out.append(
            blend_rows(
                padded[first_level:last_level],
                weights,
                first_level,
                last_level,
                displace,
                HALO,
                rows_here,
            )
        )
    advected = jnp.concatenate(pieces_out, axis=0)
    wave_y = jnp.arange(modes_y, dtype=jnp.int32)
    angle_y = phase_angles(wave_y, jnp.arange(columns, dtype=jnp.int32), columns)
    table_y = jnp.stack([jnp.cos(angle_y), -jnp.sin(angle_y)], axis=1).reshape(2 * modes_y, columns)
    flattened = advected.reshape(levels * rows_here, columns)
    coefficients = lax.dot_general(
        table_y, flattened, (((1,), (1,)), ((), ())), precision=lax.Precision.HIGHEST
    )
    coefficients = coefficients.reshape(shards, modes_here, 2, levels * rows_here)
    wave_square = ((2.0 * wave_y.astype(jnp.float32) / columns) ** 2).reshape(shards, modes_here, 1)
    index_x = jnp.arange(modes_x, dtype=jnp.int32)
    wave_x = jnp.where(index_x < modes_x // 2, index_x, index_x - modes_x)
    angle_x = phase_angles(wave_x, jnp.arange(length_x, dtype=jnp.int32), length_x)
    cosine = jnp.cos(angle_x)
    sine = jnp.sin(angle_x)
    forward_x = jnp.stack(
        [jnp.stack([cosine.T, -sine.T], axis=1), jnp.stack([sine.T, cosine.T], axis=1)], axis=1
    )
    forward_x = forward_x.reshape(shards, rows_here, 2, 2, modes_x)
    inverse_x = (
        jnp.stack([jnp.stack([cosine, sine], axis=-1), jnp.stack([-sine, cosine], axis=-1)], axis=0)
        / length_x
    )
    inverse_x = inverse_x.reshape(2, modes_x, shards, rows_here, 2)
    square_x = (2.0 * wave_x.astype(jnp.float32) / length_x) ** 2
    spectral_in = lax.all_to_all(coefficients, "gx", split_axis=0, concat_axis=0, tiled=True)
    square_in = lax.all_to_all(wave_square, "gx", split_axis=0, concat_axis=0, tiled=True)
    item_count = spectral_in.shape[1]
    blocks = spectral_in.reshape(shards, item_count, 2, levels, rows_here)
    spectra = jnp.einsum("nkplc,ncpqm->kqlm", blocks, forward_x, precision=lax.Precision.HIGHEST)
    projected = jnp.einsum(
        "al,kqlm->kqam", mode_projection, spectra, precision=lax.Precision.HIGHEST
    )
    kappa = square_in[0][:, :, None] + square_x[None, None, :]
    factor = 1.0 / (1.0 + mode_rates[None, :, None] * kappa)
    solved = jnp.einsum(
        "la,kqam->kqlm",
        vertical_modes,
        projected * factor[:, None],
        precision=lax.Precision.HIGHEST,
    )
    returned = jnp.einsum("kqlm,qmncp->nkplc", solved, inverse_x, precision=lax.Precision.HIGHEST)
    returned = returned.reshape(shards, item_count, 2, levels * rows_here)
    merged = lax.all_to_all(returned, "gx", split_axis=0, concat_axis=0, tiled=True)
    weights_y = jnp.where(wave_y == 0, 1.0, 2.0).astype(jnp.float32) / columns
    table_back = table_y * jnp.repeat(weights_y, 2)[:, None]
    updated = lax.dot_general(
        merged.reshape(2 * modes_y, levels * rows_here),
        table_back,
        (((0,), (0,)), ((), ())),
        precision=lax.Precision.HIGHEST,
    )
    return updated.reshape(levels, rows_here, columns)


CHUNK = 24
GROUP = 8
SPAN = 2 * CHUNK
PIECES = SPAN // 8
VMEM_BYTES = 56 * 1024 * 1024
BF16 = jnp.bfloat16
F32 = jnp.float32


def drift_of(level, levels):
    return (9 * level) // levels - 4


def group_drifts(group, levels):
    first = drift_of(GROUP * group, levels)
    last = drift_of(GROUP * group + GROUP - 1, levels)
    split = next(
        (s for s in range(GROUP) if drift_of(GROUP * group + s, levels) != first), GROUP
    )
    return first, last, split


def halo_groups(levels, rows_here):
    before, after = [], []
    for j in range(rows_here + 3):
        for group in range(levels // GROUP):
            first, last, _ = group_drifts(group, levels)
            if j - 2 - last < 0:
                before.append((j, group))
            if j - 2 - first >= rows_here:
                after.append((j, group))
    return before, after


def split_two(value):
    high = value.astype(BF16)
    return high, (value - high.astype(F32)).astype(BF16)


def dot3(left, right, dims):
    def dot(a, b):
        return lax.dot_general(a, b, (dims, ((), ())), preferred_element_type=F32)

    return dot(left[0], right[0]) + (dot(left[0], right[1]) + dot(left[1], right[0]))


def kernel_weights(fraction):
    p = 1.0 - fraction
    low, lower, upper = p - 1.0, p - 2.0, p + 1.0
    a, b = p * low, upper * lower
    return (
        a * lower * (-1.0 / 6.0),
        b * low * 0.5,
        b * p * (-0.5),
        a * upper * (1.0 / 6.0),
    )


def upper_mask(split, width):
    return lax.broadcasted_iota(jnp.int32, (GROUP, width), 0) >= split


def y_sweep_kernel(tracer, frac, interim, before_out, after_out):
    rows_here, levels, columns = tracer.shape
    for pair in range(levels // (2 * GROUP)):

        @pl.loop(0, rows_here)
        def _(i, pair=pair):
            fractions = frac[i, 2 * GROUP * pair : 2 * GROUP * (pair + 1), :].astype(F32)
            for half in range(2):
                group = 2 * pair + half
                first, last, split = group_drifts(group, levels)
                weights = kernel_weights(fractions[GROUP * half : GROUP * (half + 1)])
                value = tracer[i, GROUP * group : GROUP * (group + 1), :]
                rolled = [
                    pltpu.roll(value, (-(t - 2 - last)) % columns, 1)
                    for t in range(4 + last - first)
                ]
                mask = upper_mask(split, columns)
                total = None
                for tap in range(4):
                    source = rolled[tap]
                    if last != first:
                        source = jnp.where(mask, rolled[tap], rolled[tap + 1])
                    term = weights[tap] * source
                    total = term if total is None else total + term
                interim[i, GROUP * group : GROUP * (group + 1), :] = total

    before, after = halo_groups(levels, rows_here)
    for out, blocks, shift in ((before_out, before, rows_here), (after_out, after, -rows_here)):
        for at, (j, group) in enumerate(blocks):
            first, last, split = group_drifts(group, levels)
            picks = []
            for drift in (first, last):
                row = min(max(j - 2 - drift + shift, 0), rows_here - 1)
                picks.append(interim[row, GROUP * group : GROUP * (group + 1), :])
            out[GROUP * at : GROUP * (at + 1), :] = jnp.where(
                upper_mask(split, picks[0].shape[1]), picks[1], picks[0]
            )


def x_sweep_kernel(interim, frac, before_in, after_in, high_out, low_out):
    rows_here, levels, columns = interim.shape
    before, after = halo_groups(levels, rows_here)
    width = 256

    for pair in range(levels // (2 * GROUP)):

        @pl.loop(0, columns // width)
        def _(step, pair=pair):
            lanes = pl.ds(pl.multiple_of(step * width, width), width)
            windows = []
            for group in (2 * pair, 2 * pair + 1):
                first, last, split = group_drifts(group, levels)
                mask = upper_mask(split, width)
                window = []
                for j in range(rows_here + 3):
                    picks = []
                    for drift in (first, last):
                        row = j - 2 - drift
                        if row < 0:
                            at = GROUP * before.index((j, group))
                            picks.append(before_in[at : at + GROUP, lanes])
                        elif row >= rows_here:
                            at = GROUP * after.index((j, group))
                            picks.append(after_in[at : at + GROUP, lanes])
                        else:
                            at = GROUP * group
                            picks.append(interim[row, at : at + GROUP, lanes])
                    window.append(jnp.where(mask, picks[1], picks[0]))
                windows.append(window)
            for i in range(rows_here):
                at = 2 * GROUP * pair
                weights = kernel_weights(frac[i, at : at + 2 * GROUP, lanes].astype(F32))
                parts = []
                for half in range(2):
                    total = None
                    for tap in range(4):
                        term = (
                            weights[tap][GROUP * half : GROUP * (half + 1)]
                            * windows[half][i + tap]
                        )
                        total = term if total is None else total + term
                    parts.append(total)
                high, low = split_two(jnp.concatenate(parts, axis=0))
                high_out[levels * i + at : levels * i + at + 2 * GROUP, lanes] = high
                low_out[levels * i + at : levels * i + at + 2 * GROUP, lanes] = low


def pack_block(block):
    return jnp.concatenate([block[8 * g : 8 * g + 8] for g in range(PIECES)], axis=1)


def unpack_block(block):
    width = block.shape[1] // PIECES
    return jnp.concatenate([block[:, width * g : width * (g + 1)] for g in range(PIECES)], axis=0)


def forward_kernel(high, low, table_high, table_low, out):
    shards = out.shape[0]
    rows = table_high.shape[0] // 2
    for part in range(2):
        span = slice(part * rows, (part + 1) * rows)
        result = dot3(
            (table_high[span], table_low[span]), (high[...], low[...]), ((1,), (1,))
        )
        for n in range(shards // 2):
            out[part * (shards // 2) + n] = pack_block(result[SPAN * n : SPAN * n + SPAN])


def solve_kernel(
    blocks, f_high, f_low, g_high, g_low, twiddle_re, twiddle_im, project, back, kappa, rates, out
):
    shards = blocks.shape[0]
    data = jnp.concatenate([unpack_block(blocks[n]) for n in range(shards)], axis=0)
    plain = ((1,), (0,))
    mixed = dot3((f_high[...], f_low[...]), split_two(data), plain)
    half = mixed.shape[0] // 2
    real, imag = mixed[:half], mixed[half:]
    project_two = split_two(project[...])
    rate = rates[...]
    scale = kappa[:, 3:4]
    out_re = out_im = None
    for part in range(3):
        t_re, t_im = twiddle_re[part], twiddle_im[part]
        turned = (real * t_re - imag * t_im, real * t_im + imag * t_re)
        factor = scale / (1.0 + rate * kappa[:, part : part + 1])
        y_re, y_im = (dot3(split_two(u), project_two, plain) * factor for u in turned)
        a_re = y_re * t_re + y_im * t_im
        a_im = y_im * t_re - y_re * t_im
        out_re = a_re if part == 0 else out_re + a_re
        out_im = a_im if part == 0 else out_im + a_im
    back_two = split_two(back[...])
    solved = jnp.concatenate(
        [dot3(split_two(u), back_two, plain) for u in (out_re, out_im)], axis=0
    )
    result = dot3((g_high[...], g_low[...]), split_two(solved), plain)
    for n in range(shards):
        out[n] = pack_block(result[SPAN * n : SPAN * n + SPAN])


def inverse_kernel(blocks, table_high, table_low, *rest):
    out = rest[-1]
    data = jnp.concatenate([unpack_block(blocks[n]) for n in range(blocks.shape[0])], axis=0)
    high, low = split_two(data.T)
    width = 512
    for step in range(out.shape[1] // width):
        lanes = slice(step * width, (step + 1) * width)
        value = dot3((high, low), (table_high[:, lanes], table_low[:, lanes]), ((1,), (0,)))
        out[:, lanes] = value if len(rest) == 1 else value + rest[0][:, lanes]


def exchange_start(sent, received, send_sems, recv_sems, wait=False):
    shards = sent.shape[0]
    me = lax.axis_index("gx")

    @pl.loop(1, shards)
    def _(step):
        peer = lax.rem(me + step, shards)
        copy = pltpu.make_async_remote_copy(
            src_ref=sent.at[peer],
            dst_ref=received.at[me],
            send_sem=send_sems.at[step],
            recv_sem=recv_sems.at[step],
            device_id={"gx": peer},
            device_id_type=pl.DeviceIdType.MESH,
        )
        if wait:
            copy.wait()
        else:
            copy.start()

    if not wait:
        received[me] = sent[me]


def spectral_kernel(chunks, high, low, *refs):
    tables = [refs[2 * c : 2 * c + 2] for c in range(chunks)]
    constants = refs[2 * chunks : 2 * chunks + 8]
    kappas = refs[2 * chunks + 8 : 3 * chunks + 8]
    rates, out, sent, received, send_sems, recv_sems = refs[3 * chunks + 8 :]
    shards = sent.shape[2]
    me = lax.axis_index("gx")
    barrier = pltpu.get_barrier_semaphore()

    @pl.loop(1, shards)
    def _(step):
        pl.semaphore_signal(
            barrier,
            inc=1,
            device_id={"gx": lax.rem(me + step, shards)},
            device_id_type=pl.DeviceIdType.MESH,
        )

    def buffers(phase, c):
        return (r.at[phase, c] for r in (sent, received, send_sems, recv_sems))

    for c in range(chunks):
        forward_kernel(high, low, *tables[c], sent.at[0, c])
        if c == 0:
            pl.semaphore_wait(barrier, shards - 1)
        exchange_start(*buffers(0, c))
    for c in range(chunks):
        exchange_start(*buffers(0, c), wait=True)
        solve_kernel(received.at[0, c], *constants, kappas[c], rates, sent.at[1, c])
        exchange_start(*buffers(1, c))
    for c in range(chunks):
        exchange_start(*buffers(1, c), wait=True)
        inverse_kernel(received.at[1, c], *tables[c], *((out, out) if c else (out,)))


def call(kernel, shapes, flops, args, aliases=None):
    size = sum(math.prod(a.shape) * a.dtype.itemsize for a in (*args, *shapes))
    return pl.pallas_call(
        kernel,
        out_shape=shapes,
        in_specs=[pl.BlockSpec(memory_space=pltpu.VMEM)] * len(args),
        out_specs=[pl.BlockSpec(memory_space=pltpu.VMEM)] * len(shapes),
        input_output_aliases=aliases or {},
        compiler_params=pltpu.CompilerParams(vmem_limit_bytes=VMEM_BYTES),
        cost_estimate=pl.CostEstimate(flops=flops, bytes_accessed=size, transcendentals=0),
    )(*args)


def two_parts(table):
    high = table.astype(ml_dtypes.bfloat16)
    low = (table - high.astype(np.float64)).astype(ml_dtypes.bfloat16)
    return high, low


def y_table(columns, shards, modes_here):
    wave = np.arange(shards * modes_here).reshape(shards, modes_here // CHUNK, CHUNK)
    wave = wave.transpose(1, 0, 2)[..., None]
    angle = (wave * np.arange(columns) % columns) * (2.0 * np.pi / columns)
    table = np.stack([np.cos(angle), -np.sin(angle)], axis=3)
    return two_parts(table.reshape(modes_here // CHUNK, shards * CHUNK * 2, columns))


def x_tables(shards, rows_here, levels):
    n = np.arange(shards)
    angle = (n[:, None] * n[None, :] % shards) * (2.0 * np.pi / shards)
    c, s = np.cos(angle), np.sin(angle)
    forward = np.stack([np.stack([c, s], 1), np.stack([-s, c], 1)], 0)
    eye = np.eye(CHUNK)
    size = 2 * shards * CHUNK
    forward = np.einsum("pmqn,kj->pmknjq", forward, eye).reshape(size, size)
    length_x = shards * rows_here
    modes_x = length_x // 2
    m = np.arange(modes_x)
    wave = np.where(m < modes_x // 2, m, m - modes_x)
    turn = (wave[:, None] * np.arange(rows_here) % length_x) * (2.0 * np.pi / length_x)
    turn = turn.reshape(-1, shards, 1, rows_here, 1)
    shape = (turn.shape[0], shards, CHUNK, rows_here, levels)
    turn = np.broadcast_to(turn, shape).reshape(-1, shards * CHUNK, rows_here * levels)
    square = ((2.0 * wave / length_x) ** 2).reshape(-1, shards).T
    square = np.repeat(square, CHUNK, axis=0).astype(np.float32)
    return (
        two_parts(forward),
        two_parts(np.ascontiguousarray(forward.T)),
        np.cos(turn).astype(np.float32),
        (-np.sin(turn)).astype(np.float32),
        square,
    )


def body(tracer, frac_x, frac_y, vertical_modes, mode_projection, mode_rates):
    levels, rows_here, columns = tracer.shape
    shards = lax.axis_size("gx")
    length_x = rows_here * shards
    modes_y = columns // 2
    modes_here = modes_y // shards
    fits = (
        shards == 16
        and modes_here % CHUNK == 0
        and length_x // 2 == 3 * shards
        and levels % (2 * GROUP) == 0
        and levels <= 48
        and columns % 512 == 0
        and all(
            group_drifts(g, levels)[1] - group_drifts(g, levels)[0] == 1
            for g in range(levels // GROUP)
        )
    )
    if not fits:
        return plain_body(tracer, frac_x, frac_y, vertical_modes, mode_projection, mode_rates)
    lines = rows_here * levels
    chunks = modes_here // CHUNK
    before, after = halo_groups(levels, rows_here)
    interim, to_right, to_left = call(
        y_sweep_kernel,
        [
            jax.ShapeDtypeStruct((rows_here, levels, columns), F32),
            jax.ShapeDtypeStruct((GROUP * len(before), columns), F32),
            jax.ShapeDtypeStruct((GROUP * len(after), columns), F32),
        ],
        40 * lines * columns,
        (jnp.swapaxes(tracer, 0, 1), jnp.swapaxes(frac_y, 0, 1)),
    )
    up = [(i, (i + 1) % shards) for i in range(shards)]
    from_left = lax.ppermute(to_right, "gx", up)
    from_right = lax.ppermute(to_left, "gx", [(j, i) for i, j in up])
    high, low = call(
        x_sweep_kernel,
        [jax.ShapeDtypeStruct((lines, columns), BF16)] * 2,
        40 * lines * columns,
        (interim, jnp.swapaxes(frac_x, 0, 1), from_left, from_right),
    )

    t_high, t_low = y_table(columns, shards, modes_here)
    f_two, g_two, twiddle_re, twiddle_im, square_x = x_tables(shards, rows_here, levels)
    eye = jnp.eye(rows_here, dtype=F32)
    project = jnp.tile(mode_projection.T, (rows_here, rows_here))
    back = (eye[:, None, :, None] * vertical_modes.T[None, :, None, :]).reshape(lines, lines)
    rates = jnp.tile(mode_rates, rows_here)[None, :]
    kappas, tables = [], []
    for c in range(chunks):
        wave = lax.axis_index("gx") * modes_here + c * CHUNK + jnp.arange(CHUNK, dtype=jnp.int32)
        square_y = jnp.tile((2.0 * wave.astype(F32) / columns) ** 2, shards)[:, None]
        scale = jnp.where(wave == 0, 1.0, 2.0).astype(F32) / (columns * length_x)
        kappas.append(
            jnp.concatenate([square_x + square_y, jnp.tile(scale, shards)[:, None]], axis=1)
        )
        tables.append((jnp.asarray(t_high[c]), jnp.asarray(t_low[c])))

    args = (
        high,
        low,
        *(part for two in tables for part in two),
        *map(jnp.asarray, (*f_two, *g_two, twiddle_re, twiddle_im)),
        project,
        back,
        *kappas,
        rates,
    )
    buffer = pltpu.VMEM((2, chunks, shards, 8, PIECES * lines), F32)
    sems = pltpu.SemaphoreType.DMA((2, chunks, shards))
    total = pl.pallas_call(
        functools.partial(spectral_kernel, chunks),
        out_shape=jax.ShapeDtypeStruct((lines, columns), F32),
        in_specs=[pl.BlockSpec(memory_space=pltpu.VMEM)] * len(args),
        out_specs=pl.BlockSpec(memory_space=pltpu.VMEM),
        scratch_shapes=[buffer, buffer, sems, sems],
        compiler_params=pltpu.CompilerParams(
            collective_id=0, has_side_effects=True, vmem_limit_bytes=VMEM_BYTES
        ),
    )(*args)
    return jnp.swapaxes(total.reshape(rows_here, levels, columns), 0, 1)


def solution(mesh):
    placed = (
        P("member", "gx", None),
        P("member", "gx", None),
        P("member", "gx", None),
        P(),
        P(),
        P(),
    )
    return jax.shard_map(
        body, mesh=mesh, in_specs=placed, out_specs=P("member", "gx", None), check_vma=False
    )
```

```python
import functools
import math

import jax
import jax.numpy as jnp
import ml_dtypes
import numpy as np
from jax import lax
from jax.experimental import pallas as pl
from jax.experimental.pallas import tpu as pltpu
from jax.sharding import PartitionSpec as P

HALO = 6


def padded_2(value, sides, width):
    for axis, dim in sides:
        size, length = (lax.axis_size(axis), value.shape[dim])
        up = [(i, (i + 1) % size) for i in range(size)]
        down = [(j, i) for i, j in up]
        last = lax.slice_in_dim(value, length - width, length, axis=dim)
        initial = lax.slice_in_dim(value, 0, width, axis=dim)
        before = lax.ppermute(last, axis, up)
        after = lax.ppermute(initial, axis, down)
        value = jnp.concatenate([before, value, after], axis=dim)
    return value


def lagrange_weights(fraction):
    position = 1.0 - fraction.astype(jnp.float32)
    return (
        -position * (position - 1.0) * (position - 2.0) / 6.0,
        (position + 1.0) * (position - 1.0) * (position - 2.0) / 2.0,
        -(position + 1.0) * position * (position - 2.0) / 2.0,
        (position + 1.0) * position * (position - 1.0) / 6.0,
    )


def drift_classes(levels):
    bounds = []
    for category in range(9):
        first_level = (category * levels + 8) // 9
        last_level = ((category + 1) * levels + 8) // 9
        bounds.append((first_level, last_level, category - 4))
    return bounds


def sweep_columns(values, fraction):
    weights = lagrange_weights(fraction)
    pieces_out = []
    for first_level, last_level, displace in drift_classes(values.shape[0]):
        section = values[first_level:last_level]
        summed = jnp.zeros(section.shape, jnp.float32)
        for stencil in range(4):
            offset = stencil - 2 - displace
            summed = summed + weights[stencil][first_level:last_level] * jnp.roll(
                section, -offset, axis=2
            )
        pieces_out.append(summed)
    return jnp.concatenate(pieces_out, axis=0)


def blend_rows(window, weights, first_level, last_level, displace, anchor, rows_here):
    summed = jnp.zeros((last_level - first_level, rows_here, window.shape[2]), jnp.float32)
    for stencil in range(4):
        offset = anchor + stencil - 2 - displace
        summed = (
            summed
            + weights[stencil][first_level:last_level] * window[:, offset : offset + rows_here]
        )
    return summed


def phase_angles(numbers, places, length):
    phases = jnp.mod(numbers[:, None] * places[None, :], length)
    return phases.astype(jnp.float32) * (2.0 * math.pi / length)


def plain_body(tracer, frac_x, frac_y, vertical_modes, mode_projection, mode_rates):
    levels, rows_here, columns = tracer.shape
    shards = lax.axis_size("gx")
    length_x = rows_here * shards
    modes_x = length_x // 2
    modes_y = columns // 2
    modes_here = modes_y // shards
    interim = sweep_columns(tracer, frac_y)
    weights = lagrange_weights(frac_x)
    classes = drift_classes(levels)
    pieces_out = []
    padded = padded_2(interim, (("gx", 1),), HALO)
    for first_level, last_level, displace in classes:
        pieces_out.append(
            blend_rows(
                padded[first_level:last_level],
                weights,
                first_level,
                last_level,
                displace,
                HALO,
                rows_here,
            )
        )
    advected = jnp.concatenate(pieces_out, axis=0)
    wave_y = jnp.arange(modes_y, dtype=jnp.int32)
    angle_y = phase_angles(wave_y, jnp.arange(columns, dtype=jnp.int32), columns)
    table_y = jnp.stack([jnp.cos(angle_y), -jnp.sin(angle_y)], axis=1).reshape(2 * modes_y, columns)
    flattened = advected.reshape(levels * rows_here, columns)
    coefficients = lax.dot_general(
        table_y, flattened, (((1,), (1,)), ((), ())), precision=lax.Precision.HIGHEST
    )
    coefficients = coefficients.reshape(shards, modes_here, 2, levels * rows_here)
    wave_square = ((2.0 * wave_y.astype(jnp.float32) / columns) ** 2).reshape(shards, modes_here, 1)
    index_x = jnp.arange(modes_x, dtype=jnp.int32)
    wave_x = jnp.where(index_x < modes_x // 2, index_x, index_x - modes_x)
    angle_x = phase_angles(wave_x, jnp.arange(length_x, dtype=jnp.int32), length_x)
    cosine = jnp.cos(angle_x)
    sine = jnp.sin(angle_x)
    forward_x = jnp.stack(
        [jnp.stack([cosine.T, -sine.T], axis=1), jnp.stack([sine.T, cosine.T], axis=1)], axis=1
    )
    forward_x = forward_x.reshape(shards, rows_here, 2, 2, modes_x)
    inverse_x = (
        jnp.stack([jnp.stack([cosine, sine], axis=-1), jnp.stack([-sine, cosine], axis=-1)], axis=0)
        / length_x
    )
    inverse_x = inverse_x.reshape(2, modes_x, shards, rows_here, 2)
    square_x = (2.0 * wave_x.astype(jnp.float32) / length_x) ** 2
    spectral_in = lax.all_to_all(coefficients, "gx", split_axis=0, concat_axis=0, tiled=True)
    square_in = lax.all_to_all(wave_square, "gx", split_axis=0, concat_axis=0, tiled=True)
    item_count = spectral_in.shape[1]
    blocks = spectral_in.reshape(shards, item_count, 2, levels, rows_here)
    spectra = jnp.einsum("nkplc,ncpqm->kqlm", blocks, forward_x, precision=lax.Precision.HIGHEST)
    projected = jnp.einsum(
        "al,kqlm->kqam", mode_projection, spectra, precision=lax.Precision.HIGHEST
    )
    kappa = square_in[0][:, :, None] + square_x[None, None, :]
    factor = 1.0 / (1.0 + mode_rates[None, :, None] * kappa)
    solved = jnp.einsum(
        "la,kqam->kqlm",
        vertical_modes,
        projected * factor[:, None],
        precision=lax.Precision.HIGHEST,
    )
    returned = jnp.einsum("kqlm,qmncp->nkplc", solved, inverse_x, precision=lax.Precision.HIGHEST)
    returned = returned.reshape(shards, item_count, 2, levels * rows_here)
    merged = lax.all_to_all(returned, "gx", split_axis=0, concat_axis=0, tiled=True)
    weights_y = jnp.where(wave_y == 0, 1.0, 2.0).astype(jnp.float32) / columns
    table_back = table_y * jnp.repeat(weights_y, 2)[:, None]
    updated = lax.dot_general(
        merged.reshape(2 * modes_y, levels * rows_here),
        table_back,
        (((0,), (0,)), ((), ())),
        precision=lax.Precision.HIGHEST,
    )
    return updated.reshape(levels, rows_here, columns)


CHUNK = 16
GROUP = 8
SPAN = 2 * CHUNK
PIECES = SPAN // 8
VMEM_BYTES = 56 * 1024 * 1024
BF16 = jnp.bfloat16
F32 = jnp.float32


def drift_of(level, levels):
    return (9 * level) // levels - 4


def group_drifts(group, levels):
    first = drift_of(GROUP * group, levels)
    last = drift_of(GROUP * group + GROUP - 1, levels)
    split = next(
        (s for s in range(GROUP) if drift_of(GROUP * group + s, levels) != first), GROUP
    )
    return first, last, split


def halo_groups(levels, rows_here):
    before, after = [], []
    for j in range(rows_here + 3):
        for group in range(levels // GROUP):
            first, last, _ = group_drifts(group, levels)
            if j - 2 - last < 0:
                before.append((j, group))
            if j - 2 - first >= rows_here:
                after.append((j, group))
    return before, after


def split_two(value):
    high = value.astype(BF16)
    return high, (value - high.astype(F32)).astype(BF16)


def dot3(left, right, dims):
    def dot(a, b):
        return lax.dot_general(a, b, (dims, ((), ())), preferred_element_type=F32)

    return dot(left[0], right[0]) + (dot(left[0], right[1]) + dot(left[1], right[0]))


def kernel_weights(fraction):
    p = 1.0 - fraction
    low, lower, upper = p - 1.0, p - 2.0, p + 1.0
    a, b = p * low, upper * lower
    return (
        a * lower * (-1.0 / 6.0),
        b * low * 0.5,
        b * p * (-0.5),
        a * upper * (1.0 / 6.0),
    )


def upper_mask(split, width):
    return lax.broadcasted_iota(jnp.int32, (GROUP, width), 0) >= split


def y_sweep_kernel(tracer, frac, interim, before_out, after_out):
    rows_here, levels, columns = tracer.shape
    for pair in range(levels // (2 * GROUP)):

        @pl.loop(0, rows_here)
        def _(i, pair=pair):
            fractions = frac[i, 2 * GROUP * pair : 2 * GROUP * (pair + 1), :].astype(F32)
            for half in range(2):
                group = 2 * pair + half
                first, last, split = group_drifts(group, levels)
                weights = kernel_weights(fractions[GROUP * half : GROUP * (half + 1)])
                value = tracer[i, GROUP * group : GROUP * (group + 1), :]
                rolled = [
                    pltpu.roll(value, (-(t - 2 - last)) % columns, 1)
                    for t in range(4 + last - first)
                ]
                mask = upper_mask(split, columns)
                total = None
                for tap in range(4):
                    source = rolled[tap]
                    if last != first:
                        source = jnp.where(mask, rolled[tap], rolled[tap + 1])
                    term = weights[tap] * source
                    total = term if total is None else total + term
                interim[i, GROUP * group : GROUP * (group + 1), :] = total

    before, after = halo_groups(levels, rows_here)
    for out, blocks, shift in ((before_out, before, rows_here), (after_out, after, -rows_here)):
        for at, (j, group) in enumerate(blocks):
            first, last, split = group_drifts(group, levels)
            picks = []
            for drift in (first, last):
                row = min(max(j - 2 - drift + shift, 0), rows_here - 1)
                picks.append(interim[row, GROUP * group : GROUP * (group + 1), :])
            out[GROUP * at : GROUP * (at + 1), :] = jnp.where(
                upper_mask(split, picks[0].shape[1]), picks[1], picks[0]
            )


def x_sweep_kernel(interim, frac, before_in, after_in, high_out, low_out):
    rows_here, levels, columns = interim.shape
    before, after = halo_groups(levels, rows_here)
    width = 256

    for pair in range(levels // (2 * GROUP)):

        @pl.loop(0, columns // width)
        def _(step, pair=pair):
            lanes = pl.ds(pl.multiple_of(step * width, width), width)
            windows = []
            for group in (2 * pair, 2 * pair + 1):
                first, last, split = group_drifts(group, levels)
                mask = upper_mask(split, width)
                window = []
                for j in range(rows_here + 3):
                    picks = []
                    for drift in (first, last):
                        row = j - 2 - drift
                        if row < 0:
                            at = GROUP * before.index((j, group))
                            picks.append(before_in[at : at + GROUP, lanes])
                        elif row >= rows_here:
                            at = GROUP * after.index((j, group))
                            picks.append(after_in[at : at + GROUP, lanes])
                        else:
                            at = GROUP * group
                            picks.append(interim[row, at : at + GROUP, lanes])
                    window.append(jnp.where(mask, picks[1], picks[0]))
                windows.append(window)
            for i in range(rows_here):
                at = 2 * GROUP * pair
                weights = kernel_weights(frac[i, at : at + 2 * GROUP, lanes].astype(F32))
                parts = []
                for half in range(2):
                    total = None
                    for tap in range(4):
                        term = (
                            weights[tap][GROUP * half : GROUP * (half + 1)]
                            * windows[half][i + tap]
                        )
                        total = term if total is None else total + term
                    parts.append(total)
                high, low = split_two(jnp.concatenate(parts, axis=0))
                high_out[levels * i + at : levels * i + at + 2 * GROUP, lanes] = high
                low_out[levels * i + at : levels * i + at + 2 * GROUP, lanes] = low


def pack_block(block):
    return jnp.concatenate([block[8 * g : 8 * g + 8] for g in range(PIECES)], axis=1)


def unpack_block(block):
    width = block.shape[1] // PIECES
    return jnp.concatenate([block[:, width * g : width * (g + 1)] for g in range(PIECES)], axis=0)


def forward_kernel(high, low, table_high, table_low, out):
    shards = out.shape[0]
    rows = table_high.shape[0] // 2
    for part in range(2):
        span = slice(part * rows, (part + 1) * rows)
        result = dot3(
            (table_high[span], table_low[span]), (high[...], low[...]), ((1,), (1,))
        )
        for n in range(shards // 2):
            out[part * (shards // 2) + n] = pack_block(result[SPAN * n : SPAN * n + SPAN])


def solve_kernel(
    blocks, f_high, f_low, g_high, g_low, twiddle_re, twiddle_im, project, back, kappa, rates, out
):
    shards = blocks.shape[0]
    data = jnp.concatenate([unpack_block(blocks[n]) for n in range(shards)], axis=0)
    plain = ((1,), (0,))
    mixed = dot3((f_high[...], f_low[...]), split_two(data), plain)
    half = mixed.shape[0] // 2
    real, imag = mixed[:half], mixed[half:]
    project_two = split_two(project[...])
    rate = rates[...]
    scale = kappa[:, 3:4]
    out_re = out_im = None
    for part in range(3):
        t_re, t_im = twiddle_re[part], twiddle_im[part]
        turned = (real * t_re - imag * t_im, real * t_im + imag * t_re)
        factor = scale / (1.0 + rate * kappa[:, part : part + 1])
        y_re, y_im = (dot3(split_two(u), project_two, plain) * factor for u in turned)
        a_re = y_re * t_re + y_im * t_im
        a_im = y_im * t_re - y_re * t_im
        out_re = a_re if part == 0 else out_re + a_re
        out_im = a_im if part == 0 else out_im + a_im
    back_two = split_two(back[...])
    solved = jnp.concatenate(
        [dot3(split_two(u), back_two, plain) for u in (out_re, out_im)], axis=0
    )
    result = dot3((g_high[...], g_low[...]), split_two(solved), plain)
    for n in range(shards):
        out[n] = pack_block(result[SPAN * n : SPAN * n + SPAN])


def inverse_kernel(blocks, table_high, table_low, *rest):
    out = rest[-1]
    data = jnp.concatenate([unpack_block(blocks[n]) for n in range(blocks.shape[0])], axis=0)
    high, low = split_two(data.T)
    width = 512
    for step in range(out.shape[1] // width):
        lanes = slice(step * width, (step + 1) * width)
        value = dot3((high, low), (table_high[:, lanes], table_low[:, lanes]), ((1,), (0,)))
        out[:, lanes] = value if len(rest) == 1 else value + rest[0][:, lanes]


def exchange_start(sent, received, send_sems, recv_sems, wait=False):
    shards = sent.shape[0]
    me = lax.axis_index("gx")

    @pl.loop(1, shards)
    def _(step):
        peer = lax.rem(me + step, shards)
        copy = pltpu.make_async_remote_copy(
            src_ref=sent.at[peer],
            dst_ref=received.at[me],
            send_sem=send_sems.at[step],
            recv_sem=recv_sems.at[step],
            device_id={"gx": peer},
            device_id_type=pl.DeviceIdType.MESH,
        )
        if wait:
            copy.wait()
        else:
            copy.start()

    if not wait:
        received[me] = sent[me]


def spectral_kernel(chunks, high, low, *refs):
    tables = [refs[2 * c : 2 * c + 2] for c in range(chunks)]
    constants = refs[2 * chunks : 2 * chunks + 8]
    kappas = refs[2 * chunks + 8 : 3 * chunks + 8]
    rates, out, sent, received, send_sems, recv_sems = refs[3 * chunks + 8 :]
    shards = sent.shape[2]
    me = lax.axis_index("gx")
    barrier = pltpu.get_barrier_semaphore()

    @pl.loop(1, shards)
    def _(step):
        pl.semaphore_signal(
            barrier,
            inc=1,
            device_id={"gx": lax.rem(me + step, shards)},
            device_id_type=pl.DeviceIdType.MESH,
        )

    def buffers(phase, c):
        return (r.at[phase, c] for r in (sent, received, send_sems, recv_sems))

    for c in range(chunks):
        forward_kernel(high, low, *tables[c], sent.at[0, c])
        if c == 0:
            pl.semaphore_wait(barrier, shards - 1)
        exchange_start(*buffers(0, c))
    for c in range(chunks):
        exchange_start(*buffers(0, c), wait=True)
        solve_kernel(received.at[0, c], *constants, kappas[c], rates, sent.at[1, c])
        exchange_start(*buffers(1, c))
    for c in range(chunks):
        exchange_start(*buffers(1, c), wait=True)
        inverse_kernel(received.at[1, c], *tables[c], *((out, out) if c else (out,)))


def call(kernel, shapes, flops, args, aliases=None):
    size = sum(math.prod(a.shape) * a.dtype.itemsize for a in (*args, *shapes))
    return pl.pallas_call(
        kernel,
        out_shape=shapes,
        in_specs=[pl.BlockSpec(memory_space=pltpu.VMEM)] * len(args),
        out_specs=[pl.BlockSpec(memory_space=pltpu.VMEM)] * len(shapes),
        input_output_aliases=aliases or {},
        compiler_params=pltpu.CompilerParams(vmem_limit_bytes=VMEM_BYTES),
        cost_estimate=pl.CostEstimate(flops=flops, bytes_accessed=size, transcendentals=0),
    )(*args)


def two_parts(table):
    high = table.astype(ml_dtypes.bfloat16)
    low = (table - high.astype(np.float64)).astype(ml_dtypes.bfloat16)
    return high, low


def y_table(columns, shards, modes_here):
    wave = np.arange(shards * modes_here).reshape(shards, modes_here // CHUNK, CHUNK)
    wave = wave.transpose(1, 0, 2)[..., None]
    angle = (wave * np.arange(columns) % columns) * (2.0 * np.pi / columns)
    table = np.stack([np.cos(angle), -np.sin(angle)], axis=3)
    return two_parts(table.reshape(modes_here // CHUNK, shards * CHUNK * 2, columns))


def x_tables(shards, rows_here, levels):
    n = np.arange(shards)
    angle = (n[:, None] * n[None, :] % shards) * (2.0 * np.pi / shards)
    c, s = np.cos(angle), np.sin(angle)
    forward = np.stack([np.stack([c, s], 1), np.stack([-s, c], 1)], 0)
    eye = np.eye(CHUNK)
    size = 2 * shards * CHUNK
    forward = np.einsum("pmqn,kj->pmknjq", forward, eye).reshape(size, size)
    length_x = shards * rows_here
    modes_x = length_x // 2
    m = np.arange(modes_x)
    wave = np.where(m < modes_x // 2, m, m - modes_x)
    turn = (wave[:, None] * np.arange(rows_here) % length_x) * (2.0 * np.pi / length_x)
    turn = turn.reshape(-1, shards, 1, rows_here, 1)
    shape = (turn.shape[0], shards, CHUNK, rows_here, levels)
    turn = np.broadcast_to(turn, shape).reshape(-1, shards * CHUNK, rows_here * levels)
    square = ((2.0 * wave / length_x) ** 2).reshape(-1, shards).T
    square = np.repeat(square, CHUNK, axis=0).astype(np.float32)
    return (
        two_parts(forward),
        two_parts(np.ascontiguousarray(forward.T)),
        np.cos(turn).astype(np.float32),
        (-np.sin(turn)).astype(np.float32),
        square,
    )


def body(tracer, frac_x, frac_y, vertical_modes, mode_projection, mode_rates):
    levels, rows_here, columns = tracer.shape
    shards = lax.axis_size("gx")
    length_x = rows_here * shards
    modes_y = columns // 2
    modes_here = modes_y // shards
    fits = (
        shards == 16
        and modes_here % CHUNK == 0
        and length_x // 2 == 3 * shards
        and levels % (2 * GROUP) == 0
        and levels <= 48
        and columns % 512 == 0
        and all(
            group_drifts(g, levels)[1] - group_drifts(g, levels)[0] == 1
            for g in range(levels // GROUP)
        )
    )
    if not fits:
        return plain_body(tracer, frac_x, frac_y, vertical_modes, mode_projection, mode_rates)
    lines = rows_here * levels
    chunks = modes_here // CHUNK
    before, after = halo_groups(levels, rows_here)
    interim, to_right, to_left = call(
        y_sweep_kernel,
        [
            jax.ShapeDtypeStruct((rows_here, levels, columns), F32),
            jax.ShapeDtypeStruct((GROUP * len(before), columns), F32),
            jax.ShapeDtypeStruct((GROUP * len(after), columns), F32),
        ],
        40 * lines * columns,
        (jnp.swapaxes(tracer, 0, 1), jnp.swapaxes(frac_y, 0, 1)),
    )
    up = [(i, (i + 1) % shards) for i in range(shards)]
    from_left = lax.ppermute(to_right, "gx", up)
    from_right = lax.ppermute(to_left, "gx", [(j, i) for i, j in up])
    high, low = call(
        x_sweep_kernel,
        [jax.ShapeDtypeStruct((lines, columns), BF16)] * 2,
        40 * lines * columns,
        (interim, jnp.swapaxes(frac_x, 0, 1), from_left, from_right),
    )

    t_high, t_low = y_table(columns, shards, modes_here)
    f_two, g_two, twiddle_re, twiddle_im, square_x = x_tables(shards, rows_here, levels)
    eye = jnp.eye(rows_here, dtype=F32)
    project = jnp.tile(mode_projection.T, (rows_here, rows_here))
    back = (eye[:, None, :, None] * vertical_modes.T[None, :, None, :]).reshape(lines, lines)
    rates = jnp.tile(mode_rates, rows_here)[None, :]
    kappas, tables = [], []
    for c in range(chunks):
        wave = lax.axis_index("gx") * modes_here + c * CHUNK + jnp.arange(CHUNK, dtype=jnp.int32)
        square_y = jnp.tile((2.0 * wave.astype(F32) / columns) ** 2, shards)[:, None]
        scale = jnp.where(wave == 0, 1.0, 2.0).astype(F32) / (columns * length_x)
        kappas.append(
            jnp.concatenate([square_x + square_y, jnp.tile(scale, shards)[:, None]], axis=1)
        )
        tables.append((jnp.asarray(t_high[c]), jnp.asarray(t_low[c])))

    args = (
        high,
        low,
        *(part for two in tables for part in two),
        *map(jnp.asarray, (*f_two, *g_two, twiddle_re, twiddle_im)),
        project,
        back,
        *kappas,
        rates,
    )
    buffer = pltpu.VMEM((2, chunks, shards, 8, PIECES * lines), F32)
    sems = pltpu.SemaphoreType.DMA((2, chunks, shards))
    total = pl.pallas_call(
        functools.partial(spectral_kernel, chunks),
        out_shape=jax.ShapeDtypeStruct((lines, columns), F32),
        in_specs=[pl.BlockSpec(memory_space=pltpu.VMEM)] * len(args),
        out_specs=pl.BlockSpec(memory_space=pltpu.VMEM),
        scratch_shapes=[buffer, buffer, sems, sems],
        compiler_params=pltpu.CompilerParams(
            collective_id=0, has_side_effects=True, vmem_limit_bytes=VMEM_BYTES
        ),
    )(*args)
    return jnp.swapaxes(total.reshape(rows_here, levels, columns), 0, 1)


def solution(mesh):
    placed = (
        P("member", "gx", None),
        P("member", "gx", None),
        P("member", "gx", None),
        P(),
        P(),
        P(),
    )
    return jax.shard_map(
        body, mesh=mesh, in_specs=placed, out_specs=P("member", "gx", None), check_vma=False
    )
```
